1024 devices in a mesh: row: 64 (over x, y), col: 16 (over z, core).
Axes of the slice: x: 8, y: 8, z: 8, core: 2. Of those that a mesh axis runs over, the one named last changes fastest.
Arguments:
- source_feats: bfloat16 [32768, 256], P(('col', 'row')), may hold values from -6 to 6
- target_feats: bfloat16 [131072, 256], P(('row', 'col')), may hold values from -6 to 6
- w_neigh: bfloat16 [256, 256], replicated, may hold values from -0.375 to 0.375
- w_self: bfloat16 [256, 256], replicated, may hold values from -0.375 to 0.375
- tile_count: int32 [64, 16], P('row', 'col'), may hold values from 1 to 48, as said below
- tile_rows: int32 [64, 16, 48], P('row', 'col'), may hold values from 0 to 15, as said below
- tile_cols: int32 [64, 16, 48], P('row', 'col'), may hold values from 0 to 15, as said below
- tile_vals: bfloat16 [64, 16, 48, 128, 128], P('row', 'col'), may hold values from -0.15625 to 0.15625
- cotangent: bfloat16 [131072, 256], P(('row', 'col')), may hold values from -6 to 6
Outputs:
- layer_out: bfloat16 [131072, 256], P(('row', 'col'))
- d_target: bfloat16 [131072, 256], P(('row', 'col'))
- d_source: bfloat16 [32768, 256], P(('col', 'row'))
- grad_neigh: float32 [256, 256], replicated
- grad_self: float32 [256, 256], replicated
The draws below stay inside these ranges and needn't reach their ends.
Inputs may be any that keep to these rules, and one draw needn't show every extreme that they name: `tile_count`: every block has between 1 and 48 live slots, and some block has exactly 48. `tile_rows`: together with tile_cols, the slots of one block name distinct tile positions. `tile_cols`: together with tile_rows, the slots of one block name distinct tile positions.
All inputs are finite; a program needn't handle non-finite values.
Results may differ from the reference program's by a relative error of at most 0.0062.
Values may be sent and summed in bfloat16 or wider, within the bound.
No kernel may reach another device: no remote copies, remote signals or barrier semaphores. Data moves between devices by JAX's collectives and lax.ppermute only.
A program may use at most 64 MiB of HBM per device.

```python
from functools import partial
import jax
import jax.numpy as jnp
from jax import lax

F = 256
TILE = 128
RB = 16
CB = 16
TILES_DEV = 48
NT = 131072
NS = 32768
N_ROW = 64
N_COL = 16


def tile_layout(key):
    block_keys = jax.random.split(key, N_ROW * N_COL)
    orders = jax.vmap(partial(jax.random.permutation, x=RB * CB))(block_keys)
    return orders[:, :TILES_DEV].reshape(N_ROW, N_COL, TILES_DEV).astype(jnp.int32)


def draw_tile_rows(key, part):
    placed = tile_layout(key)
    return (placed // CB).astype(jnp.int32)


def draw_tile_cols(key, part):
    placed = tile_layout(key)
    return (placed % CB).astype(jnp.int32)


def draw_tile_count(key, part):
    key = jax.random.fold_in(key, 13)
    key_one, key_two, key_three = jax.random.split(key, 3)
    left_part = jax.random.randint(key_one, (N_ROW * N_COL,), 0, TILES_DEV)
    right_part = jax.random.randint(key_two, (N_ROW * N_COL,), 0, TILES_DEV)
    counts = 1 + left_part * right_part // TILES_DEV
    fullest = jax.random.randint(key_three, (), 0, N_ROW * N_COL)
    counts = jnp.where(jnp.arange(N_ROW * N_COL, dtype=jnp.int32) == fullest, TILES_DEV, counts)
    return counts.reshape(N_ROW, N_COL).astype(jnp.int32)


def block_scale(own_key, dims, cuts, least, top_value):
    def one(axis_at, parts):
        steps = jax.random.uniform(jax.random.fold_in(jax.random.fold_in(own_key, 6), axis_at), (parts,), jnp.float32, least / len(cuts), top_value / len(cuts))
        return jnp.repeat(jnp.exp(steps), dims[axis_at] // parts).reshape((-1,) + (1,) * (len(dims) - axis_at - 1))

    gain = one(*cuts[0])
    for cut in cuts[1:]:
        gain = gain * one(*cut)
    return gain


def centred(rng, dims, scale, limit, cuts=(), kind=jnp.bfloat16):
    entries = jax.random.normal(rng, dims, jnp.float32) * scale
    if len(cuts) > 0:
        entries = block_scale(rng, dims, cuts, -0.22, 0.18) * entries
    return jnp.clip(entries, min=-limit, max=limit).astype(kind)


def setup_inputs(seed: int = 0) -> dict:
    keys = jax.random.split(jax.random.key(seed), 10)
    source_feats = centred(keys[0], (NS, F), 1.0, 6.0, ((0, 1024),))
    target_feats = centred(keys[1], (NT, F), 1.0, 6.0, ((0, 1024),))
    w_neigh = centred(keys[2], (F, F), F ** -0.5, 0.375)
    w_self = centred(keys[3], (F, F), F ** -0.5, 0.375)
    tile_count = draw_tile_count(jax.random.fold_in(keys[9], 71), 0)
    tile_rows = draw_tile_rows(jax.random.fold_in(keys[9], 71), 0)
    tile_cols = draw_tile_cols(jax.random.fold_in(keys[9], 71), 0)
    tile_vals = centred(keys[7], (N_ROW, N_COL, TILES_DEV, TILE, TILE), (N_COL * TILE * TILES_DEV // (4 * RB)) ** -0.5, 0.15625, ((0, 64), (1, 16)))
    cotangent = centred(keys[8], (NT, F), 1.0, 6.0, ((0, 1024),))
    return {"source_feats": source_feats, "target_feats": target_feats, "w_neigh": w_neigh, "w_self": w_self, "tile_count": tile_count, "tile_rows": tile_rows, "tile_cols": tile_cols, "tile_vals": tile_vals, "cotangent": cotangent}


def gelu_parts(preact):
    normal_cdf = 0.5 * (1.0 + jax.scipy.special.erf(preact * 0.7071067811865476))
    density = jnp.exp(-0.5 * preact * preact) * 0.3989422804014327
    return preact * normal_cdf, normal_cdf + preact * density


def reference(source_feats, target_feats, w_neigh, w_self, tile_count, tile_rows, tile_cols, tile_vals, cotangent):
    width = source_feats.shape[1]
    slot_count = tile_vals.shape[2]
    tile_size = tile_vals.shape[3]
    live_mask = (jnp.arange(slot_count, dtype=jnp.int32)[None, None, :] < tile_count[:, :, None]).astype(jnp.float32)
    row_pick = (tile_rows[..., None] == jnp.arange(RB, dtype=jnp.int32)).astype(jnp.float32) * live_mask[..., None]
    col_pick = (tile_cols[..., None] == jnp.arange(CB, dtype=jnp.int32)).astype(jnp.float32) * live_mask[..., None]
    source_tiles = source_feats.reshape(N_COL, CB, tile_size, width)
    col_index = jnp.arange(N_COL, dtype=jnp.int32)[:, None]

    def forward_block(inputs):
        values, columns, picks = inputs
        picked = source_tiles[col_index, columns]
        products = jnp.einsum('csij,csjf->csif', values.astype(jnp.float32), picked.astype(jnp.float32), precision=lax.Precision.HIGHEST)
        summed = jnp.einsum('csr,csif->rif', picks, products, precision=lax.Precision.HIGHEST)
        return summed.reshape(RB * tile_size, width)

    partial_rows = lax.map(forward_block, (tile_vals, tile_cols, row_pick))
    aggregate = partial_rows.reshape(NT, width).astype(jnp.bfloat16)
    preact = jnp.dot(aggregate, w_neigh, preferred_element_type=jnp.float32) + jnp.dot(target_feats, w_self, preferred_element_type=jnp.float32)
    activated, slope = gelu_parts(preact)
    layer_out = activated.astype(jnp.bfloat16)
    d_preact = (cotangent.astype(jnp.float32) * slope).astype(jnp.bfloat16)
    grad_neigh = jnp.dot(aggregate.T, d_preact, preferred_element_type=jnp.float32)
    grad_self = jnp.dot(target_feats.T, d_preact, preferred_element_type=jnp.float32)
    d_aggregate = jnp.dot(d_preact, w_neigh.T, preferred_element_type=jnp.float32).astype(jnp.bfloat16)
    d_target = jnp.dot(d_preact, w_self.T, preferred_element_type=jnp.float32).astype(jnp.bfloat16)
    d_blocks = d_aggregate.reshape(N_ROW, RB, tile_size, width)

    def backward_block(carry, inputs):
        values, rows_here, picks, grads_here = inputs
        picked = grads_here[rows_here]
        products = jnp.einsum('csji,csjf->csif', values.astype(jnp.float32), picked.astype(jnp.float32), precision=lax.Precision.HIGHEST)
        added = jnp.einsum('csk,csif->ckif', picks, products, precision=lax.Precision.HIGHEST)
        return carry + added, None

    initial = jnp.zeros((N_COL, CB, tile_size, width), jnp.float32)
    total, unused = lax.scan(backward_block, initial, (tile_vals, tile_rows, col_pick, d_blocks))
    d_source = total.reshape(NS, width).astype(jnp.bfloat16)
    return layer_out, d_target, d_source, grad_neigh, grad_self
```

```python
import jax
import jax.numpy as jnp
from jax import lax
from jax.experimental import pallas as pl
from jax.experimental.pallas import tpu as pltpu
from jax.sharding import PartitionSpec as P

RB = 16
CB = 16
TILE = 128
GROUP = 4
F32 = jnp.float32
BF16 = jnp.bfloat16
VMEM = pl.BlockSpec(memory_space=pltpu.VMEM)
SMEM = pl.BlockSpec(memory_space=pltpu.SMEM)
PARAMS = pltpu.CompilerParams(vmem_limit_bytes=32 * 1024 * 1024)


def live_groups(count_ref):
    return (count_ref[0, 0] + (GROUP - 1)) // GROUP


def forward_tiles(count_ref, rows_ref, cols_ref, vals_ref, src_ref, out_ref, total):
    count = count_ref[0, 0]
    total[...] = jnp.zeros_like(total)

    def group(g, carry):
        for k in range(GROUP):
            s = g * GROUP + k
            at = pl.ds(pl.multiple_of(rows_ref[0, 0, s] * TILE, TILE), TILE)
            of = pl.ds(pl.multiple_of(cols_ref[0, 0, s] * TILE, TILE), TILE)
            product = jnp.dot(vals_ref[0, 0, s], src_ref[of, :], preferred_element_type=F32)
            total[at, :] += jnp.where(s < count, product, 0.0)
        return carry

    lax.fori_loop(0, live_groups(count_ref), group, 0)
    out_ref[...] = total[...].astype(BF16)


def backward_tiles(
    count_ref, rows_ref, cols_ref, vals_ref, d_pre_ref, w_neigh_ref, out_ref, d_agg, total
):
    count = count_ref[0, 0]
    total[...] = jnp.zeros_like(total)
    d_agg[...] = lax.dot_general(
        d_pre_ref[...], w_neigh_ref[...], (((1,), (1,)), ((), ())), preferred_element_type=F32
    ).astype(BF16)

    def group(g, carry):
        for k in range(GROUP):
            s = g * GROUP + k
            of = pl.ds(pl.multiple_of(rows_ref[0, 0, s] * TILE, TILE), TILE)
            at = pl.ds(pl.multiple_of(cols_ref[0, 0, s] * TILE, TILE), TILE)
            product = lax.dot_general(
                vals_ref[0, 0, s], d_agg[of, :], (((0,), (0,)), ((), ())), preferred_element_type=F32
            )
            total[at, :] += jnp.where(s < count, product, 0.0)
        return carry

    lax.fori_loop(0, live_groups(count_ref), group, 0)
    out_ref[...] = total[...].astype(BF16)


def dense_step(
    parts_ref, own_ref, cot_ref, w_neigh_ref, w_self_ref, out_ref, d_tgt_ref, d_pre_ref, feats_ref
):
    agg = jnp.sum(parts_ref[...].astype(F32), axis=0).astype(BF16)
    own = own_ref[...]
    preact = jnp.dot(agg, w_neigh_ref[...], preferred_element_type=F32) + jnp.dot(
        own, w_self_ref[...], preferred_element_type=F32
    )
    cdf = 0.5 * (1.0 + lax.erf(preact * 0.7071067811865476))
    density = jnp.exp(-0.5 * preact * preact) * 0.3989422804014327
    out_ref[...] = (preact * cdf).astype(BF16)
    d_pre = (cot_ref[...].astype(F32) * (cdf + preact * density)).astype(BF16)
    d_pre_ref[...] = d_pre
    d_tgt_ref[...] = lax.dot_general(
        d_pre, w_self_ref[...], (((1,), (1,)), ((), ())), preferred_element_type=F32
    ).astype(BF16)
    width = own.shape[1]
    feats_ref[:width, :] = agg.T
    feats_ref[width:, :] = own.T


def grad_step(feats_ref, d_pre_ref, out_ref):
    n, rows, _ = feats_ref.shape
    total = jnp.zeros(out_ref.shape, F32)
    for k in range(n):
        total += jnp.dot(
            feats_ref[k], d_pre_ref[k * TILE : (k + 1) * TILE, :], preferred_element_type=F32
        )
    out_ref[...] = total


def sum_step(parts_ref, out_ref):
    out_ref[...] = jnp.sum(parts_ref[...].astype(F32), axis=0).astype(BF16)


def call(kernel, ins, outs, scratch=()):
    single = not isinstance(outs, list)
    return pl.pallas_call(
        kernel,
        out_shape=outs,
        in_specs=ins,
        out_specs=VMEM if single else [VMEM] * len(outs),
        scratch_shapes=scratch,
        compiler_params=PARAMS,
    )


def on_device(
    source_feats, target_feats, w_neigh, w_self, tile_count, tile_rows, tile_cols, tile_vals, cotangent
):
    width = source_feats.shape[1]
    n_col = lax.axis_size("col")
    n_row = lax.axis_size("row")
    own_rows = target_feats.shape[0]
    sds = jax.ShapeDtypeStruct
    slots = [SMEM, SMEM, SMEM, VMEM]

    block_source = lax.all_gather(source_feats, "row", axis=0, tiled=True)
    partial_rows = call(
        forward_tiles, slots + [VMEM], sds((RB * TILE, width), BF16),
        [pltpu.VMEM((RB * TILE, width), F32)],
    )(tile_count, tile_rows, tile_cols, tile_vals, block_source)
    parts = lax.all_to_all(partial_rows, "col", 0, 0, tiled=True)
    layer_out, d_target, d_preact, feats = call(
        dense_step, [VMEM] * 5,
        [sds((own_rows, width), BF16)] * 3 + [sds((2 * width, own_rows), BF16)],
    )(parts.reshape(n_col, own_rows, width), target_feats, cotangent, w_neigh, w_self)

    d_pre_block = lax.all_gather(d_preact, "col", axis=0, tiled=True)
    share = width // n_col
    feats = feats.reshape(2, n_col, share, own_rows).swapaxes(0, 1).reshape(2 * width, own_rows)
    feat_parts = lax.all_to_all(feats, "col", 0, 0, tiled=True)
    grads = call(grad_step, [VMEM] * 2, sds((2 * share, width), F32))(
        feat_parts.reshape(n_col, 2 * share, own_rows), d_pre_block
    )
    source_part = call(
        backward_tiles, slots + [VMEM, VMEM], sds((CB * TILE, width), BF16),
        [pltpu.VMEM((RB * TILE, width), BF16), pltpu.VMEM((CB * TILE, width), F32)],
    )(tile_count, tile_rows, tile_cols, tile_vals, d_pre_block, w_neigh)
    source_parts = lax.all_to_all(source_part, "row", 0, 0, tiled=True)
    d_source = call(sum_step, [VMEM], sds(source_feats.shape, BF16))(
        source_parts.reshape(n_row, -1, width)
    )
    grads = lax.psum(grads, "row")
    grads = lax.all_gather(grads, "col", axis=0, tiled=False)
    grads = grads.reshape(n_col, 2, share, width).swapaxes(0, 1).reshape(2, width, width)
    return (layer_out, d_target, d_source, grads[0], grads[1])


def solution(mesh):
    in_specs = (
        P(("col", "row"), None),
        P(("row", "col"), None),
        P(),
        P(),
        P("row", "col"),
        P("row", "col", None),
        P("row", "col", None),
        P("row", "col", None, None, None),
        P(("row", "col"), None),
    )
    out_specs = (
        P(("row", "col"), None),
        P(("row", "col"), None),
        P(("col", "row"), None),
        P(),
        P(),
    )
    return jax.shard_map(
        on_device, mesh=mesh, in_specs=in_specs, out_specs=out_specs, check_vma=False
    )
```

```python
import jax
import jax.numpy as jnp
from jax import lax
from jax.experimental import pallas as pl
from jax.experimental.pallas import tpu as pltpu
from jax.sharding import Mesh, PartitionSpec as P

RB = 16
CB = 16
TILE = 128
GROUP = 4
SHARE = 16
TAIL = 16
ROW = ("x", "y")
COL = ("z", "core")
F32 = jnp.float32
BF16 = jnp.bfloat16
VMEM = pl.BlockSpec(memory_space=pltpu.VMEM)
SMEM = pl.BlockSpec(memory_space=pltpu.SMEM)
PARAMS = pltpu.CompilerParams(vmem_limit_bytes=32 * 1024 * 1024)


def live_groups(count_ref):
    return (count_ref[0, 0] + (GROUP - 1)) // GROUP


def forward_tiles(
    core_ref, count_ref, rows_ref, cols_ref, vals_ref, src_ref, mine_ref, send_ref, total
):
    count = count_ref[0, 0]
    total[...] = jnp.zeros_like(total)

    def group(g, carry):
        for k in range(GROUP):
            s = g * GROUP + k
            at = pl.ds(pl.multiple_of(rows_ref[0, 0, s] * TILE, TILE), TILE)
            of = pl.ds(pl.multiple_of(cols_ref[0, 0, s] * TILE, TILE), TILE)
            product = jnp.dot(vals_ref[0, 0, s], src_ref[of, :], preferred_element_type=F32)
            total[at, :] += jnp.where(s < count, product, 0.0)
        return carry

    lax.fori_loop(0, live_groups(count_ref), group, 0)
    core = core_ref[0, 0]
    share = mine_ref.shape[0] // (RB // 2)
    for k in range(RB // 2):
        here = slice(k * share, (k + 1) * share)
        keep = pl.ds(pl.multiple_of((2 * k + core) * share, share), share)
        give = pl.ds(pl.multiple_of((2 * k + 1 - core) * share, share), share)
        mine_ref[here, :] = total[keep, :]
        send_ref[here, :] = total[give, :].astype(BF16)


def assemble(head_ref, swap_ref, d_pre):
    n = swap_ref.shape[0]
    head = head_ref.shape[0] // n
    full = head + TAIL
    half = d_pre.shape[1] // 2
    for k in range(n):
        d_pre[k * full : k * full + head, :] = head_ref[k * head : (k + 1) * head, :]
        rows = slice(k * full + head, (k + 1) * full)
        d_pre[rows, :half] = swap_ref[k, 2 * SHARE : 2 * SHARE + TAIL, :]
        d_pre[rows, half:] = swap_ref[k, 2 * SHARE + TAIL : 2 * SHARE + 2 * TAIL, :]


def backward_tiles(
    count_ref, rows_ref, cols_ref, vals_ref, head_ref, swap_ref, w_neigh_ref, out_ref,
    d_pre, d_agg, total,
):
    count = count_ref[0, 0]
    total[...] = jnp.zeros_like(total)
    assemble(head_ref, swap_ref, d_pre)
    d_agg[...] = lax.dot_general(
        d_pre[...], w_neigh_ref[...], (((1,), (1,)), ((), ())), preferred_element_type=F32
    ).astype(BF16)

    def group(g, carry):
        for k in range(GROUP):
            s = g * GROUP + k
            of = pl.ds(pl.multiple_of(rows_ref[0, 0, s] * TILE, TILE), TILE)
            at = pl.ds(pl.multiple_of(cols_ref[0, 0, s] * TILE, TILE), TILE)
            product = lax.dot_general(
                vals_ref[0, 0, s], d_agg[of, :], (((0,), (0,)), ((), ())), preferred_element_type=F32
            )
            total[at, :] += jnp.where(s < count, product, 0.0)
        return carry

    lax.fori_loop(0, live_groups(count_ref), group, 0)
    out_ref[...] = total[...].astype(BF16)


def dense_step(
    parts_ref, own_ref, cot_ref, w_neigh_ref, w_self_ref, out_ref, d_tgt_ref, head_ref, swap_ref
):
    agg = jnp.sum(parts_ref[...].astype(F32), axis=0).astype(BF16)
    own = own_ref[...]
    preact = jnp.dot(agg, w_neigh_ref[...], preferred_element_type=F32) + jnp.dot(
        own, w_self_ref[...], preferred_element_type=F32
    )
    cdf = 0.5 * (1.0 + lax.erf(preact * 0.7071067811865476))
    density = jnp.exp(-0.5 * preact * preact) * 0.3989422804014327
    out_ref[...] = (preact * cdf).astype(BF16)
    d_pre = (cot_ref[...].astype(F32) * (cdf + preact * density)).astype(BF16)
    d_tgt_ref[...] = lax.dot_general(
        d_pre, w_self_ref[...], (((1,), (1,)), ((), ())), preferred_element_type=F32
    ).astype(BF16)
    head = head_ref.shape[0]
    half = d_pre.shape[1] // 2
    head_ref[...] = d_pre[:head, :]
    agg_t = agg.T
    own_t = own.T
    for k in range(swap_ref.shape[0]):
        swap_ref[k, :SHARE, :] = agg_t[k * SHARE : (k + 1) * SHARE, :]
        swap_ref[k, SHARE : 2 * SHARE, :] = own_t[k * SHARE : (k + 1) * SHARE, :]
        swap_ref[k, 2 * SHARE : 2 * SHARE + TAIL, :] = d_pre[head:, :half]
        swap_ref[k, 2 * SHARE + TAIL :, :] = d_pre[head:, half:]


def grad_step(head_ref, swap_ref, out_ref, d_pre):
    assemble(head_ref, swap_ref, d_pre)
    n = swap_ref.shape[0]
    total = jnp.zeros((2 * SHARE, d_pre.shape[1]), F32)
    for k in range(n):
        total += jnp.dot(
            swap_ref[k, : 2 * SHARE, :], d_pre[k * TILE : (k + 1) * TILE, :],
            preferred_element_type=F32,
        )
    out_ref[...] = total


def sum_step(parts_ref, out_ref):
    out_ref[...] = jnp.sum(parts_ref[...].astype(F32), axis=0).astype(BF16)


def call(kernel, ins, outs, scratch=()):
    single = not isinstance(outs, list)
    return pl.pallas_call(
        kernel,
        out_shape=outs,
        in_specs=ins,
        out_specs=VMEM if single else [VMEM] * len(outs),
        scratch_shapes=scratch,
        compiler_params=PARAMS,
    )


def on_device(
    source_feats, target_feats, w_neigh, w_self, tile_count, tile_rows, tile_cols, tile_vals, cotangent
):
    width = source_feats.shape[1]
    n_x, n_y, n_z = (lax.axis_size(a) for a in ("x", "y", "z"))
    n_col = lax.axis_size(COL)
    n_row = lax.axis_size(ROW)
    own_rows = target_feats.shape[0]
    own_source = source_feats.shape[0]
    sds = jax.ShapeDtypeStruct
    slots = [SMEM, SMEM, SMEM, VMEM]
    rows = RB * TILE

    block_source = lax.all_to_all(
        jnp.broadcast_to(source_feats[None], (n_row, own_source, width)), ROW, 0, 0, tiled=True
    ).reshape(rows, width)
    core = lax.axis_index("core").astype(jnp.int32).reshape(1, 1)
    mine, send = call(
        forward_tiles, [SMEM] + slots + [VMEM],
        [sds((rows // 2, width), F32), sds((rows // 2, width), BF16)],
        [pltpu.VMEM((rows, width), F32)],
    )(core, tile_count, tile_rows, tile_cols, tile_vals, block_source)
    got = lax.ppermute(send, "core", [(0, 1), (1, 0)])
    pair = (mine + got.astype(F32)).astype(BF16)
    parts = lax.all_to_all(pair, "z", 0, 0, tiled=True)
    layer_out, d_target, head, swap = call(
        dense_step, [VMEM] * 5,
        [sds((own_rows, width), BF16)] * 2
        + [sds((own_rows - TAIL, width), BF16), sds((n_col, 2 * SHARE + 2 * TAIL, own_rows), BF16)],
    )(parts.reshape(n_z, own_rows, width), target_feats, cotangent, w_neigh, w_self)

    swapped = lax.all_to_all(swap, COL, 0, 0, tiled=True)
    heads = lax.all_gather(head, COL, axis=0, tiled=True)
    grads = call(
        grad_step, [VMEM] * 2, sds((2 * SHARE, width), F32),
        [pltpu.VMEM((rows, width), BF16)],
    )(heads, swapped)
    grads_y = lax.all_to_all(
        jnp.broadcast_to(grads[None], (n_y,) + grads.shape), "y", 0, 0, tiled=True
    )
    source_part = call(
        backward_tiles, slots + [VMEM] * 3, sds((CB * TILE, width), BF16),
        [pltpu.VMEM((rows, width), BF16)] * 2 + [pltpu.VMEM((CB * TILE, width), F32)],
    )(tile_count, tile_rows, tile_cols, tile_vals, heads, swapped, w_neigh)
    source_parts = lax.all_to_all(source_part, ROW, 0, 0, tiled=True)
    grads = jnp.sum(grads_y, axis=0)
    grads_x = lax.all_gather(grads, ("x", "core"), axis=0, tiled=False)
    grads_x = grads_x.reshape((n_x, 2) + grads.shape)
    grads = jnp.sum(lax.dynamic_index_in_dim(grads_x, core[0, 0], 1, keepdims=False), axis=0)
    all_grads = lax.all_gather(grads, COL, axis=0, tiled=False)
    d_source = call(sum_step, [VMEM], sds(source_feats.shape, BF16))(
        source_parts.reshape(n_row, -1, width)
    )
    all_grads = all_grads.reshape(n_col, 2, SHARE, width).swapaxes(0, 1).reshape(2, width, width)
    return (layer_out, d_target, d_source, all_grads[0], all_grads[1])


def solution(mesh):
    n_row, n_col = mesh.devices.shape
    n_y = min(n_row, 8)
    mesh = Mesh(mesh.devices.reshape(n_row // n_y, n_y, n_col // 2, 2), ROW + COL)
    targets = P(ROW + COL, None)
    sources = P(COL + ROW, None)
    in_specs = (
        sources,
        targets,
        P(),
        P(),
        P(ROW, COL),
        P(ROW, COL, None),
        P(ROW, COL, None),
        P(ROW, COL, None, None, None),
        targets,
    )
    out_specs = (targets, targets, sources, P(), P())
    return jax.shard_map(
        on_device, mesh=mesh, in_specs=in_specs, out_specs=out_specs, check_vma=False
    )
```

```python
import jax
import jax.numpy as jnp
from jax import lax
from jax.experimental import pallas as pl
from jax.experimental.pallas import tpu as pltpu
from jax.sharding import Mesh, PartitionSpec as P

RB = 16
CB = 16
TILE = 128
GROUP = 4
SHARE = 16
TAIL = 16
ROW = ("x", "y")
COL = ("z", "core")
F32 = jnp.float32
BF16 = jnp.bfloat16
VMEM = pl.BlockSpec(memory_space=pltpu.VMEM)
SMEM = pl.BlockSpec(memory_space=pltpu.SMEM)
PARAMS = pltpu.CompilerParams(vmem_limit_bytes=32 * 1024 * 1024)


def live_groups(count_ref):
    return (count_ref[0, 0] + (GROUP - 1)) // GROUP


def forward_tiles(
    core_ref, count_ref, rows_ref, cols_ref, vals_ref, src_ref, mine_ref, send_ref, total
):
    count = count_ref[0, 0]
    total[...] = jnp.zeros_like(total)

    def group(g, carry):
        for k in range(GROUP):
            s = g * GROUP + k
            at = pl.ds(pl.multiple_of(rows_ref[0, 0, s] * TILE, TILE), TILE)
            of = pl.ds(pl.multiple_of(cols_ref[0, 0, s] * TILE, TILE), TILE)
            product = jnp.dot(vals_ref[0, 0, s], src_ref[of, :], preferred_element_type=F32)
            total[at, :] += jnp.where(s < count, product, 0.0)
        return carry

    lax.fori_loop(0, live_groups(count_ref), group, 0)
    core = core_ref[0, 0]
    share = mine_ref.shape[0] // (RB // 2)
    for k in range(RB // 2):
        here = slice(k * share, (k + 1) * share)
        keep = pl.ds(pl.multiple_of((2 * k + core) * share, share), share)
        give = pl.ds(pl.multiple_of((2 * k + 1 - core) * share, share), share)
        mine_ref[here, :] = total[keep, :]
        send_ref[here, :] = total[give, :].astype(BF16)


def assemble(head_ref, swap_ref, d_pre):
    n = swap_ref.shape[0]
    head = head_ref.shape[0] // n
    full = head + TAIL
    half = d_pre.shape[1] // 2
    for k in range(n):
        d_pre[k * full : k * full + head, :] = head_ref[k * head : (k + 1) * head, :]
        rows = slice(k * full + head, (k + 1) * full)
        d_pre[rows, :half] = swap_ref[k, 2 * SHARE : 2 * SHARE + TAIL, :]
        d_pre[rows, half:] = swap_ref[k, 2 * SHARE + TAIL : 2 * SHARE + 2 * TAIL, :]


def backward_tiles(
    count_ref, rows_ref, cols_ref, vals_ref, head_ref, swap_ref, w_neigh_ref, after_ref, out_ref,
    d_pre, d_agg, total,
):
    count = count_ref[0, 0]
    total[...] = jnp.zeros_like(total)
    assemble(head_ref, swap_ref, d_pre)
    d_agg[...] = lax.dot_general(
        d_pre[...], w_neigh_ref[...], (((1,), (1,)), ((), ())), preferred_element_type=F32
    ).astype(BF16)

    def group(g, carry):
        for k in range(GROUP):
            s = g * GROUP + k
            of = pl.ds(pl.multiple_of(rows_ref[0, 0, s] * TILE, TILE), TILE)
            at = pl.ds(pl.multiple_of(cols_ref[0, 0, s] * TILE, TILE), TILE)
            product = lax.dot_general(
                vals_ref[0, 0, s], d_agg[of, :], (((0,), (0,)), ((), ())), preferred_element_type=F32
            )
            total[at, :] += jnp.where(s < count, product, 0.0)
        return carry

    lax.fori_loop(0, live_groups(count_ref), group, 0)
    out_ref[...] = total[...].astype(BF16)


def dense_step(
    parts_ref, own_ref, cot_ref, w_neigh_ref, w_self_ref, out_ref, d_tgt_ref, head_ref, swap_ref
):
    agg = jnp.sum(parts_ref[...].astype(F32), axis=0).astype(BF16)
    own = own_ref[...]
    preact = jnp.dot(agg, w_neigh_ref[...], preferred_element_type=F32) + jnp.dot(
        own, w_self_ref[...], preferred_element_type=F32
    )
    cdf = 0.5 * (1.0 + lax.erf(preact * 0.7071067811865476))
    density = jnp.exp(-0.5 * preact * preact) * 0.3989422804014327
    out_ref[...] = (preact * cdf).astype(BF16)
    d_pre = (cot_ref[...].astype(F32) * (cdf + preact * density)).astype(BF16)
    d_tgt_ref[...] = lax.dot_general(
        d_pre, w_self_ref[...], (((1,), (1,)), ((), ())), preferred_element_type=F32
    ).astype(BF16)
    head = head_ref.shape[0]
    half = d_pre.shape[1] // 2
    head_ref[...] = d_pre[:head, :]
    agg_t = agg.T
    own_t = own.T
    for k in range(swap_ref.shape[0]):
        swap_ref[k, :SHARE, :] = agg_t[k * SHARE : (k + 1) * SHARE, :]
        swap_ref[k, SHARE : 2 * SHARE, :] = own_t[k * SHARE : (k + 1) * SHARE, :]
        swap_ref[k, 2 * SHARE : 2 * SHARE + TAIL, :] = d_pre[head:, :half]
        swap_ref[k, 2 * SHARE + TAIL :, :] = d_pre[head:, half:]


def grad_step(head_ref, swap_ref, out_ref, d_pre):
    assemble(head_ref, swap_ref, d_pre)
    n = swap_ref.shape[0]
    total = jnp.zeros((2 * SHARE, d_pre.shape[1]), F32)
    for k in range(n):
        total += jnp.dot(
            swap_ref[k, : 2 * SHARE, :], d_pre[k * TILE : (k + 1) * TILE, :],
            preferred_element_type=F32,
        )
    for k in range(out_ref.shape[0]):
        out_ref[k] = total


def repeat_step(one_ref, out_ref):
    one = one_ref[...]
    for k in range(out_ref.shape[0]):
        out_ref[k] = one


def sum_repeat_step(parts_ref, out_ref):
    total = jnp.sum(parts_ref[...], axis=0)
    for k in range(out_ref.shape[0]):
        out_ref[k] = total


def sum_step(parts_ref, out_ref):
    out_ref[...] = jnp.sum(parts_ref[...].astype(F32), axis=0).astype(BF16)


def call(kernel, ins, outs, scratch=()):
    single = not isinstance(outs, list)
    return pl.pallas_call(
        kernel,
        out_shape=outs,
        in_specs=ins,
        out_specs=VMEM if single else [VMEM] * len(outs),
        scratch_shapes=scratch,
        compiler_params=PARAMS,
    )


def on_device(
    source_feats, target_feats, w_neigh, w_self, tile_count, tile_rows, tile_cols, tile_vals, cotangent
):
    width = source_feats.shape[1]
    n_x, n_y, n_z = (lax.axis_size(a) for a in ("x", "y", "z"))
    n_col = lax.axis_size(COL)
    n_row = lax.axis_size(ROW)
    own_rows = target_feats.shape[0]
    own_source = source_feats.shape[0]
    sds = jax.ShapeDtypeStruct
    slots = [SMEM, SMEM, SMEM, VMEM]
    rows = RB * TILE

    block_source = lax.all_to_all(
        call(repeat_step, [VMEM], sds((n_row, own_source, width), BF16))(source_feats),
        ROW, 0, 0, tiled=True,
    ).reshape(rows, width)
    core = lax.axis_index("core").astype(jnp.int32).reshape(1, 1)
    mine, send = call(
        forward_tiles, [SMEM] + slots + [VMEM],
        [sds((rows // 2, width), F32), sds((rows // 2, width), BF16)],
        [pltpu.VMEM((rows, width), F32)],
    )(core, tile_count, tile_rows, tile_cols, tile_vals, block_source)
    got = lax.ppermute(send, "core", [(0, 1), (1, 0)])
    pair = (mine + got.astype(F32)).astype(BF16)
    parts = lax.all_to_all(pair, "z", 0, 0, tiled=True)
    layer_out, d_target, head, swap = call(
        dense_step, [VMEM] * 5,
        [sds((own_rows, width), BF16)] * 2
        + [sds((own_rows - TAIL, width), BF16), sds((n_col, 2 * SHARE + 2 * TAIL, own_rows), BF16)],
    )(parts.reshape(n_z, own_rows, width), target_feats, cotangent, w_neigh, w_self)

    swapped = lax.all_to_all(swap, COL, 0, 0, tiled=True)
    heads = lax.all_gather(head, COL, axis=0, tiled=True)
    grads = call(
        grad_step, [VMEM] * 2, sds((n_y, 2 * SHARE, width), F32),
        [pltpu.VMEM((rows, width), BF16)],
    )(heads, swapped)
    grads = lax.all_to_all(grads, "y", 0, 0, tiled=True)
    grads = call(sum_repeat_step, [VMEM], sds((n_x, 2 * SHARE, width), F32))(grads)
    grads_x = lax.all_to_all(grads, "x", 0, 0, tiled=True)
    source_part = call(
        backward_tiles, slots + [VMEM] * 3 + [pl.BlockSpec(memory_space=pl.ANY)], sds((CB * TILE, width), BF16),
        [pltpu.VMEM((rows, width), BF16)] * 2 + [pltpu.VMEM((CB * TILE, width), F32)],
    )(tile_count, tile_rows, tile_cols, tile_vals, heads, swapped, w_neigh, grads)
    source_parts = lax.all_to_all(source_part, ROW, 0, 0, tiled=True)
    grads = jnp.sum(grads_x, axis=0)
    all_grads = lax.all_gather(grads, COL, axis=0, tiled=False)
    d_source = call(sum_step, [VMEM], sds(source_feats.shape, BF16))(
        source_parts.reshape(n_row, -1, width)
    )
    all_grads = all_grads.reshape(n_col, 2, SHARE, width).swapaxes(0, 1).reshape(2, width, width)
    return (layer_out, d_target, d_source, all_grads[0], all_grads[1])


def solution(mesh):
    n_row, n_col = mesh.devices.shape
    n_y = min(n_row, 8)
    mesh = Mesh(mesh.devices.reshape(n_row // n_y, n_y, n_col // 2, 2), ROW + COL)
    targets = P(ROW + COL, None)
    sources = P(COL + ROW, None)
    in_specs = (
        sources,
        targets,
        P(),
        P(),
        P(ROW, COL),
        P(ROW, COL, None),
        P(ROW, COL, None),
        P(ROW, COL, None, None, None),
        targets,
    )
    out_specs = (targets, targets, sources, P(), P())
    return jax.shard_map(
        on_device, mesh=mesh, in_specs=in_specs, out_specs=out_specs, check_vma=False
    )
```

```python
import jax
import jax.numpy as jnp
from jax import lax
from jax.experimental import pallas as pl
from jax.experimental.pallas import tpu as pltpu
from jax.sharding import Mesh, PartitionSpec as P

RB = 16
CB = 16
TILE = 128
GROUP = 4
SHARE = 16
TAIL = 16
ROW = ("x", "y")
COL = ("z", "core")
F32 = jnp.float32
BF16 = jnp.bfloat16
VMEM = pl.BlockSpec(memory_space=pltpu.VMEM)
SMEM = pl.BlockSpec(memory_space=pltpu.SMEM)
PARAMS = pltpu.CompilerParams(vmem_limit_bytes=32 * 1024 * 1024)


def live_groups(count_ref):
    return (count_ref[0, 0] + (GROUP - 1)) // GROUP


def forward_tiles(
    core_ref, count_ref, rows_ref, cols_ref, vals_ref, src_ref, mine_ref, send_ref, total
):
    count = count_ref[0, 0]
    total[...] = jnp.zeros_like(total)

    def group(g, carry):
        for k in range(GROUP):
            s = g * GROUP + k
            at = pl.ds(pl.multiple_of(rows_ref[0, 0, s] * TILE, TILE), TILE)
            of = pl.ds(pl.multiple_of(cols_ref[0, 0, s] * TILE, TILE), TILE)
            product = jnp.dot(vals_ref[0, 0, s], src_ref[of, :], preferred_element_type=F32)
            total[at, :] += jnp.where(s < count, product, 0.0)
        return carry

    lax.fori_loop(0, live_groups(count_ref), group, 0)
    core = core_ref[0, 0]
    share = mine_ref.shape[0] // (RB // 2)
    for k in range(RB // 2):
        here = slice(k * share, (k + 1) * share)
        keep = pl.ds(pl.multiple_of((2 * k + core) * share, share), share)
        give = pl.ds(pl.multiple_of((2 * k + 1 - core) * share, share), share)
        mine_ref[here, :] = total[keep, :]
        send_ref[here, :] = total[give, :].astype(BF16)


def assemble(head_ref, swap_ref, d_pre):
    n = swap_ref.shape[0]
    head = head_ref.shape[0] // n
    full = head + TAIL
    half = d_pre.shape[1] // 2
    for k in range(n):
        d_pre[k * full : k * full + head, :] = head_ref[k * head : (k + 1) * head, :]
        rows = slice(k * full + head, (k + 1) * full)
        d_pre[rows, :half] = swap_ref[k, 2 * SHARE : 2 * SHARE + TAIL, :]
        d_pre[rows, half:] = swap_ref[k, 2 * SHARE + TAIL : 2 * SHARE + 2 * TAIL, :]


def backward_tiles(
    count_ref, rows_ref, cols_ref, vals_ref, head_ref, swap_ref, w_neigh_ref, after_ref, out_ref,
    d_pre, d_agg, total,
):
    count = count_ref[0, 0]
    total[...] = jnp.zeros_like(total)
    assemble(head_ref, swap_ref, d_pre)
    d_agg[...] = lax.dot_general(
        d_pre[...], w_neigh_ref[...], (((1,), (1,)), ((), ())), preferred_element_type=F32
    ).astype(BF16)

    def group(g, carry):
        for k in range(GROUP):
            s = g * GROUP + k
            of = pl.ds(pl.multiple_of(rows_ref[0, 0, s] * TILE, TILE), TILE)
            at = pl.ds(pl.multiple_of(cols_ref[0, 0, s] * TILE, TILE), TILE)
            product = lax.dot_general(
                vals_ref[0, 0, s], d_agg[of, :], (((0,), (0,)), ((), ())), preferred_element_type=F32
            )
            total[at, :] += jnp.where(s < count, product, 0.0)
        return carry

    lax.fori_loop(0, live_groups(count_ref), group, 0)
    out_ref[...] = total[...].astype(BF16)


def dense_step(
    parts_ref, own_ref, cot_ref, w_neigh_ref, w_self_ref, out_ref, d_tgt_ref, head_ref, swap_ref
):
    agg = jnp.sum(parts_ref[...].astype(F32), axis=0).astype(BF16)
    own = own_ref[...]
    preact = jnp.dot(agg, w_neigh_ref[...], preferred_element_type=F32) + jnp.dot(
        own, w_self_ref[...], preferred_element_type=F32
    )
    cdf = 0.5 * (1.0 + lax.erf(preact * 0.7071067811865476))
    density = jnp.exp(-0.5 * preact * preact) * 0.3989422804014327
    out_ref[...] = (preact * cdf).astype(BF16)
    d_pre = (cot_ref[...].astype(F32) * (cdf + preact * density)).astype(BF16)
    d_tgt_ref[...] = lax.dot_general(
        d_pre, w_self_ref[...], (((1,), (1,)), ((), ())), preferred_element_type=F32
    ).astype(BF16)
    head = head_ref.shape[0]
    half = d_pre.shape[1] // 2
    head_ref[...] = d_pre[:head, :]
    agg_t = agg.T
    own_t = own.T
    for k in range(swap_ref.shape[0]):
        swap_ref[k, :SHARE, :] = agg_t[k * SHARE : (k + 1) * SHARE, :]
        swap_ref[k, SHARE : 2 * SHARE, :] = own_t[k * SHARE : (k + 1) * SHARE, :]
        swap_ref[k, 2 * SHARE : 2 * SHARE + TAIL, :] = d_pre[head:, :half]
        swap_ref[k, 2 * SHARE + TAIL :, :] = d_pre[head:, half:]


def grad_step(head_ref, swap_ref, out_ref, d_pre):
    assemble(head_ref, swap_ref, d_pre)
    n = swap_ref.shape[0]
    total = jnp.zeros((2 * SHARE, d_pre.shape[1]), F32)
    for k in range(n):
        total += jnp.dot(
            swap_ref[k, : 2 * SHARE, :], d_pre[k * TILE : (k + 1) * TILE, :],
            preferred_element_type=F32,
        )
    for k in range(out_ref.shape[0]):
        out_ref[k] = total


def repeat_step(one_ref, out_ref):
    one = one_ref[...]
    for k in range(out_ref.shape[0]):
        out_ref[k] = one


def sum_step(parts_ref, out_ref):
    out_ref[...] = jnp.sum(parts_ref[...].astype(F32), axis=0).astype(BF16)


def call(kernel, ins, outs, scratch=()):
    single = not isinstance(outs, list)
    return pl.pallas_call(
        kernel,
        out_shape=outs,
        in_specs=ins,
        out_specs=VMEM if single else [VMEM] * len(outs),
        scratch_shapes=scratch,
        compiler_params=PARAMS,
    )


def on_device(
    source_feats, target_feats, w_neigh, w_self, tile_count, tile_rows, tile_cols, tile_vals, cotangent
):
    width = source_feats.shape[1]
    n_x, n_y, n_z = (lax.axis_size(a) for a in ("x", "y", "z"))
    n_col = lax.axis_size(COL)
    n_row = lax.axis_size(ROW)
    own_rows = target_feats.shape[0]
    own_source = source_feats.shape[0]
    sds = jax.ShapeDtypeStruct
    slots = [SMEM, SMEM, SMEM, VMEM]
    rows = RB * TILE

    block_source = lax.all_to_all(
        call(repeat_step, [VMEM], sds((n_row, own_source, width), BF16))(source_feats),
        ROW, 0, 0, tiled=True,
    ).reshape(rows, width)
    core = lax.axis_index("core").astype(jnp.int32).reshape(1, 1)
    mine, send = call(
        forward_tiles, [SMEM] + slots + [VMEM],
        [sds((rows // 2, width), F32), sds((rows // 2, width), BF16)],
        [pltpu.VMEM((rows, width), F32)],
    )(core, tile_count, tile_rows, tile_cols, tile_vals, block_source)
    got = lax.ppermute(send, "core", [(0, 1), (1, 0)])
    pair = (mine + got.astype(F32)).astype(BF16)
    parts = lax.all_to_all(pair, "z", 0, 0, tiled=True)
    layer_out, d_target, head, swap = call(
        dense_step, [VMEM] * 5,
        [sds((own_rows, width), BF16)] * 2
        + [sds((own_rows - TAIL, width), BF16), sds((n_col, 2 * SHARE + 2 * TAIL, own_rows), BF16)],
    )(parts.reshape(n_z, own_rows, width), target_feats, cotangent, w_neigh, w_self)

    swapped = lax.all_to_all(swap, COL, 0, 0, tiled=True)
    heads = lax.all_gather(head, COL, axis=0, tiled=True)
    grads_own = call(
        grad_step, [VMEM] * 2, sds((n_y, 2 * SHARE, width), F32),
        [pltpu.VMEM((rows, width), BF16)],
    )(heads, swapped)
    grads = lax.psum_scatter(
        grads_own.reshape(-1, width), "y", scatter_dimension=0, tiled=True
    )
    grads = call(repeat_step, [VMEM], sds((n_x, 2 * SHARE, width), F32))(grads)
    grads = lax.psum_scatter(
        grads.reshape(-1, width), "x", scatter_dimension=0, tiled=True
    )
    source_part = call(
        backward_tiles, slots + [VMEM] * 3 + [pl.BlockSpec(memory_space=pl.ANY)], sds((CB * TILE, width), BF16),
        [pltpu.VMEM((rows, width), BF16)] * 2 + [pltpu.VMEM((CB * TILE, width), F32)],
    )(tile_count, tile_rows, tile_cols, tile_vals, heads, swapped, w_neigh, grads_own)
    source_parts = lax.all_to_all(source_part, ROW, 0, 0, tiled=True)
    all_grads = lax.all_gather(grads, COL, axis=0, tiled=False)
    d_source = call(sum_step, [VMEM], sds(source_feats.shape, BF16))(
        source_parts.reshape(n_row, -1, width)
    )
    all_grads = all_grads.reshape(n_col, 2, SHARE, width).swapaxes(0, 1).reshape(2, width, width)
    return (layer_out, d_target, d_source, all_grads[0], all_grads[1])


def solution(mesh):
    n_row, n_col = mesh.devices.shape
    n_y = min(n_row, 8)
    mesh = Mesh(mesh.devices.reshape(n_row // n_y, n_y, n_col // 2, 2), ROW + COL)
    targets = P(ROW + COL, None)
    sources = P(COL + ROW, None)
    in_specs = (
        sources,
        targets,
        P(),
        P(),
        P(ROW, COL),
        P(ROW, COL, None),
        P(ROW, COL, None),
        P(ROW, COL, None, None, None),
        targets,
    )
    out_specs = (targets, targets, sources, P(), P())
    return jax.shard_map(
        on_device, mesh=mesh, in_specs=in_specs, out_specs=out_specs, check_vma=False
    )
```

```python
import jax
import jax.numpy as jnp
from jax import lax
from jax.experimental import pallas as pl
from jax.experimental.pallas import tpu as pltpu
from jax.sharding import Mesh, PartitionSpec as P

RB = 16
CB = 16
TILE = 128
GROUP = 4
SHARE = 16
TAIL = 16
ROW = ("x", "y")
COL = ("z", "core")
F32 = jnp.float32
BF16 = jnp.bfloat16
VMEM = pl.BlockSpec(memory_space=pltpu.VMEM)
SMEM = pl.BlockSpec(memory_space=pltpu.SMEM)
ANY = pl.BlockSpec(memory_space=pl.ANY)
PARAMS = pltpu.CompilerParams(vmem_limit_bytes=32 * 1024 * 1024)


def live_groups(count_ref):
    return (count_ref[0, 0] + (GROUP - 1)) // GROUP


def forward_tiles(
    core_ref, count_ref, rows_ref, cols_ref, vals_ref, src_ref, mine_ref, send_ref, total
):
    count = count_ref[0, 0]
    total[...] = jnp.zeros_like(total)

    def group(g, carry):
        for k in range(GROUP):
            s = g * GROUP + k
            at = pl.ds(pl.multiple_of(rows_ref[0, 0, s] * TILE, TILE), TILE)
            of = pl.ds(pl.multiple_of(cols_ref[0, 0, s] * TILE, TILE), TILE)
            product = jnp.dot(vals_ref[0, 0, s], src_ref[of, :], preferred_element_type=F32)
            total[at, :] += jnp.where(s < count, product, 0.0)
        return carry

    lax.fori_loop(0, live_groups(count_ref), group, 0)
    core = core_ref[0, 0]
    share = mine_ref.shape[0] // (RB // 2)
    for k in range(RB // 2):
        here = slice(k * share, (k + 1) * share)
        keep = pl.ds(pl.multiple_of((2 * k + core) * share, share), share)
        give = pl.ds(pl.multiple_of((2 * k + 1 - core) * share, share), share)
        mine_ref[here, :] = total[keep, :]
        send_ref[here, :] = total[give, :].astype(BF16)


def assemble(head_ref, swap_ref, d_pre):
    n = swap_ref.shape[0]
    head = head_ref.shape[0] // n
    full = head + TAIL
    half = d_pre.shape[1] // 2
    for k in range(n):
        d_pre[k * full : k * full + head, :] = head_ref[k * head : (k + 1) * head, :]
        rows = slice(k * full + head, (k + 1) * full)
        d_pre[rows, :half] = swap_ref[k, 2 * SHARE : 2 * SHARE + TAIL, :]
        d_pre[rows, half:] = swap_ref[k, 2 * SHARE + TAIL : 2 * SHARE + 2 * TAIL, :]


def backward_tiles(
    count_ref, rows_ref, cols_ref, vals_ref, head_ref, swap_ref, w_neigh_ref, out_ref,
    d_pre, d_agg, total,
):
    count = count_ref[0, 0]
    total[...] = jnp.zeros_like(total)
    assemble(head_ref, swap_ref, d_pre)
    d_agg[...] = lax.dot_general(
        d_pre[...], w_neigh_ref[...], (((1,), (1,)), ((), ())), preferred_element_type=F32
    ).astype(BF16)

    def group(g, carry):
        for k in range(GROUP):
            s = g * GROUP + k
            of = pl.ds(pl.multiple_of(rows_ref[0, 0, s] * TILE, TILE), TILE)
            at = pl.ds(pl.multiple_of(cols_ref[0, 0, s] * TILE, TILE), TILE)
            product = lax.dot_general(
                vals_ref[0, 0, s], d_agg[of, :], (((0,), (0,)), ((), ())), preferred_element_type=F32
            )
            total[at, :] += jnp.where(s < count, product, 0.0)
        return carry

    lax.fori_loop(0, live_groups(count_ref), group, 0)
    n = out_ref.shape[0]
    share = total.shape[0] // n
    for k in range(n):
        out_ref[k, :share, :] = total[k * share : (k + 1) * share, :].astype(BF16)
        out_ref[k, share:, :] = jnp.zeros((out_ref.shape[1] - share, total.shape[1]), BF16)


def dense_step(
    parts_ref, own_ref, cot_ref, w_neigh_ref, w_self_ref, out_ref, d_tgt_ref, head_ref, swap_ref
):
    agg = jnp.sum(parts_ref[...].astype(F32), axis=0).astype(BF16)
    own = own_ref[...]
    preact = jnp.dot(agg, w_neigh_ref[...], preferred_element_type=F32) + jnp.dot(
        own, w_self_ref[...], preferred_element_type=F32
    )
    cdf = 0.5 * (1.0 + lax.erf(preact * 0.7071067811865476))
    density = jnp.exp(-0.5 * preact * preact) * 0.3989422804014327
    out_ref[...] = (preact * cdf).astype(BF16)
    d_pre = (cot_ref[...].astype(F32) * (cdf + preact * density)).astype(BF16)
    d_tgt_ref[...] = lax.dot_general(
        d_pre, w_self_ref[...], (((1,), (1,)), ((), ())), preferred_element_type=F32
    ).astype(BF16)
    head = head_ref.shape[0]
    half = d_pre.shape[1] // 2
    head_ref[...] = d_pre[:head, :]
    agg_t = agg.T
    own_t = own.T
    for k in range(swap_ref.shape[0]):
        swap_ref[k, :SHARE, :] = agg_t[k * SHARE : (k + 1) * SHARE, :]
        swap_ref[k, SHARE : 2 * SHARE, :] = own_t[k * SHARE : (k + 1) * SHARE, :]
        swap_ref[k, 2 * SHARE : 2 * SHARE + TAIL, :] = d_pre[head:, :half]
        swap_ref[k, 2 * SHARE + TAIL :, :] = d_pre[head:, half:]


def grad_step(head_ref, swap_ref, out_ref, d_pre):
    assemble(head_ref, swap_ref, d_pre)
    n = swap_ref.shape[0]
    total = jnp.zeros((2 * SHARE, d_pre.shape[1]), F32)
    for k in range(n):
        total += jnp.dot(
            swap_ref[k, : 2 * SHARE, :], d_pre[k * TILE : (k + 1) * TILE, :],
            preferred_element_type=F32,
        )
    for k in range(out_ref.shape[0]):
        out_ref[k] = total


def repeat_step(one_ref, out_ref, sems):
    copies = [
        pltpu.make_async_copy(one_ref, out_ref.at[k], sems.at[k]) for k in range(out_ref.shape[0])
    ]
    for copy in copies:
        copy.start()
    for copy in copies:
        copy.wait()


def place_step(parts_ref, blocks_ref, out_ref, total, sems):
    del blocks_ref
    n = out_ref.shape[0]
    rows = total.shape[0]
    first = out_ref.shape[1] - rows
    total[...] = jnp.sum(parts_ref[...], axis=0).astype(BF16)
    copies = [
        pltpu.make_async_copy(total, out_ref.at[k, pl.ds(first, rows)], sems.at[k])
        for k in range(n)
    ]
    for copy in copies:
        copy.start()
    for copy in copies:
        copy.wait()


def stage_sum(parts_ref, source_ref):
    rows = source_ref.shape[0]
    source_ref[...] = jnp.sum(parts_ref[:, :rows, :].astype(F32), axis=0).astype(BF16)


def split_grads(parts_ref, after_ref, neigh_ref, self_ref):
    del after_ref
    for k in range(parts_ref.shape[0]):
        rows = slice(k * SHARE, (k + 1) * SHARE)
        neigh_ref[rows, :] = parts_ref[k, :SHARE, :]
        self_ref[rows, :] = parts_ref[k, SHARE:, :]


def stage_grads(parts_ref, after_ref, grads_ref):
    del after_ref
    rows = grads_ref.shape[0]
    grads_ref[...] = jnp.sum(parts_ref[:, parts_ref.shape[1] - rows :, :].astype(F32), axis=0)


def sum_step(parts_ref, out_ref):
    out_ref[...] = jnp.sum(parts_ref[...].astype(F32), axis=0).astype(BF16)


def call(kernel, ins, outs, scratch=(), out_spec=VMEM, aliases=None):
    single = not isinstance(outs, list)
    return pl.pallas_call(
        kernel,
        out_shape=outs,
        in_specs=ins,
        out_specs=out_spec if single else [out_spec] * len(outs),
        scratch_shapes=scratch,
        input_output_aliases=aliases or {},
        compiler_params=PARAMS,
    )


def on_device(
    source_feats, target_feats, w_neigh, w_self, tile_count, tile_rows, tile_cols, tile_vals, cotangent
):
    width = source_feats.shape[1]
    n_x, n_y, n_z = (lax.axis_size(a) for a in ("x", "y", "z"))
    n_col = lax.axis_size(COL)
    n_row = lax.axis_size(ROW)
    own_rows = target_feats.shape[0]
    own_source = source_feats.shape[0]
    sds = jax.ShapeDtypeStruct
    slots = [SMEM, SMEM, SMEM, VMEM]
    rows = RB * TILE

    block_source = lax.all_to_all(
        call(
            repeat_step, [ANY], sds((n_row, own_source, width), BF16),
            [pltpu.SemaphoreType.DMA((n_row,))], ANY,
        )(source_feats),
        ROW, 0, 0, tiled=True,
    ).reshape(rows, width)
    core = lax.axis_index("core").astype(jnp.int32).reshape(1, 1)
    mine, send = call(
        forward_tiles, [SMEM] + slots + [VMEM],
        [sds((rows // 2, width), F32), sds((rows // 2, width), BF16)],
        [pltpu.VMEM((rows, width), F32)],
    )(core, tile_count, tile_rows, tile_cols, tile_vals, block_source)
    got = lax.ppermute(send, "core", [(0, 1), (1, 0)])
    pair = (mine + got.astype(F32)).astype(BF16)
    parts = lax.all_to_all(pair, "z", 0, 0, tiled=True)
    layer_out, d_target, head, swap = call(
        dense_step, [VMEM] * 5,
        [sds((own_rows, width), BF16)] * 2
        + [sds((own_rows - TAIL, width), BF16), sds((n_col, 2 * SHARE + 2 * TAIL, own_rows), BF16)],
    )(parts.reshape(n_z, own_rows, width), target_feats, cotangent, w_neigh, w_self)

    swapped = lax.all_to_all(swap, COL, 0, 0, tiled=True)
    heads = lax.all_gather(head, COL, axis=0, tiled=True)
    grads = call(
        grad_step, [VMEM] * 2, sds((n_y, 2 * SHARE, width), F32),
        [pltpu.VMEM((rows, width), BF16)],
    )(heads, swapped)
    grads_y = lax.all_to_all(grads, "y", 0, 0, tiled=True)
    blocks = call(
        backward_tiles, slots + [VMEM] * 3,
        sds((n_x, rows // n_x + 2 * SHARE, width), BF16),
        [pltpu.VMEM((rows, width), BF16)] * 2 + [pltpu.VMEM((CB * TILE, width), F32)],
    )(tile_count, tile_rows, tile_cols, tile_vals, heads, swapped, w_neigh)
    blocks = call(
        place_step, [VMEM, ANY], sds(blocks.shape, BF16),
        [pltpu.VMEM((2 * SHARE, width), BF16), pltpu.SemaphoreType.DMA((n_x,))], ANY, {1: 0},
    )(grads_y, blocks)
    blocks = lax.all_to_all(blocks, "x", 0, 0, tiled=True)
    source_y = call(stage_sum, [VMEM], sds((rows // n_x, width), BF16))(blocks)
    grads = call(stage_grads, [VMEM, ANY], sds((2 * SHARE, width), F32))(blocks, source_y)
    source_parts = lax.all_to_all(source_y, "y", 0, 0, tiled=True)
    all_grads = lax.all_gather(grads, COL, axis=0, tiled=False)
    d_source = call(sum_step, [VMEM], sds(source_feats.shape, BF16))(
        source_parts.reshape(n_y, -1, width)
    )
    grad_neigh, grad_self = call(
        split_grads, [VMEM, ANY], [sds((width, width), F32)] * 2
    )(all_grads, d_source)
    return (layer_out, d_target, d_source, grad_neigh, grad_self)


def solution(mesh):
    n_row, n_col = mesh.devices.shape
    n_y = min(n_row, 8)
    mesh = Mesh(mesh.devices.reshape(n_row // n_y, n_y, n_col // 2, 2), ROW + COL)
    targets = P(ROW + COL, None)
    sources = P(COL + ROW, None)
    in_specs = (
        sources,
        targets,
        P(),
        P(),
        P(ROW, COL),
        P(ROW, COL, None),
        P(ROW, COL, None),
        P(ROW, COL, None, None, None),
        targets,
    )
    out_specs = (targets, targets, sources, P(), P())
    return jax.shard_map(
        on_device, mesh=mesh, in_specs=in_specs, out_specs=out_specs, check_vma=False
    )
```

```python
import jax
import jax.numpy as jnp
from jax import lax
from jax.experimental import pallas as pl
from jax.experimental.pallas import tpu as pltpu
from jax.sharding import Mesh, PartitionSpec as P

RB = 16
CB = 16
TILE = 128
GROUP = 16
REST = 8
SHARE = 16
TAIL = 16
ROW = ("x", "y")
COL = ("z", "core")
F32 = jnp.float32
BF16 = jnp.bfloat16
VMEM = pl.BlockSpec(memory_space=pltpu.VMEM)
SMEM = pl.BlockSpec(memory_space=pltpu.SMEM)
PARAMS = pltpu.CompilerParams(vmem_limit_bytes=32 * 1024 * 1024)


def live_tiles(count, add, product):
    groups = count // GROUP
    done = groups * GROUP

    def group(g, carry):
        for k in range(GROUP):
            s = g * GROUP + k
            add(s, product(s))
        return carry

    def rest(g, carry):
        for k in range(REST):
            s = done + g * REST + k
            add(s, jnp.where(s < count, product(s), 0.0))
        return carry

    lax.fori_loop(0, groups, group, 0)
    lax.fori_loop(0, (count - done + (REST - 1)) // REST, rest, 0)


def forward_tiles(
    core_ref, count_ref, rows_ref, cols_ref, vals_ref, src_ref, mine_ref, send_ref, total
):
    count = count_ref[0, 0]
    total[...] = jnp.zeros_like(total)

    def product(s):
        of = pl.ds(pl.multiple_of(cols_ref[0, 0, s] * TILE, TILE), TILE)
        return jnp.dot(vals_ref[0, 0, s], src_ref[of, :], preferred_element_type=F32)

    def add(s, value):
        at = pl.ds(pl.multiple_of(rows_ref[0, 0, s] * TILE, TILE), TILE)
        total[at, :] += value

    live_tiles(count, add, product)
    core = core_ref[0, 0]
    share = mine_ref.shape[0] // (RB // 2)
    for k in range(RB // 2):
        here = slice(k * share, (k + 1) * share)
        keep = pl.ds(pl.multiple_of((2 * k + core) * share, share), share)
        give = pl.ds(pl.multiple_of((2 * k + 1 - core) * share, share), share)
        mine_ref[here, :] = total[keep, :]
        send_ref[here, :] = total[give, :].astype(BF16)


def assemble(head_ref, swap_ref, d_pre):
    n = swap_ref.shape[0]
    head = head_ref.shape[0] // n
    full = head + TAIL
    half = d_pre.shape[1] // 2
    for k in range(n):
        d_pre[k * full : k * full + head, :] = head_ref[k * head : (k + 1) * head, :]
        rows = slice(k * full + head, (k + 1) * full)
        d_pre[rows, :half] = swap_ref[k, 2 * SHARE : 2 * SHARE + TAIL, :]
        d_pre[rows, half:] = swap_ref[k, 2 * SHARE + TAIL : 2 * SHARE + 2 * TAIL, :]


def backward_tiles(
    count_ref, rows_ref, cols_ref, vals_ref, head_ref, swap_ref, w_neigh_ref, after_ref, out_ref,
    d_pre, d_agg, total,
):
    count = count_ref[0, 0]
    total[...] = jnp.zeros_like(total)
    assemble(head_ref, swap_ref, d_pre)
    d_agg[...] = lax.dot_general(
        d_pre[...], w_neigh_ref[...], (((1,), (1,)), ((), ())), preferred_element_type=F32
    ).astype(BF16)

    def product(s):
        of = pl.ds(pl.multiple_of(rows_ref[0, 0, s] * TILE, TILE), TILE)
        return lax.dot_general(
            vals_ref[0, 0, s], d_agg[of, :], (((0,), (0,)), ((), ())), preferred_element_type=F32
        )

    def add(s, value):
        at = pl.ds(pl.multiple_of(cols_ref[0, 0, s] * TILE, TILE), TILE)
        total[at, :] += value

    live_tiles(count, add, product)
    out_ref[...] = total[...].astype(BF16)


def dense_step(
    parts_ref, own_ref, cot_ref, w_neigh_ref, w_self_ref, out_ref, d_tgt_ref, head_ref, swap_ref
):
    agg = jnp.sum(parts_ref[...].astype(F32), axis=0).astype(BF16)
    own = own_ref[...]
    preact = jnp.dot(agg, w_neigh_ref[...], preferred_element_type=F32) + jnp.dot(
        own, w_self_ref[...], preferred_element_type=F32
    )
    cdf = 0.5 * (1.0 + lax.erf(preact * 0.7071067811865476))
    density = jnp.exp(-0.5 * preact * preact) * 0.3989422804014327
    out_ref[...] = (preact * cdf).astype(BF16)
    d_pre = (cot_ref[...].astype(F32) * (cdf + preact * density)).astype(BF16)
    d_tgt_ref[...] = lax.dot_general(
        d_pre, w_self_ref[...], (((1,), (1,)), ((), ())), preferred_element_type=F32
    ).astype(BF16)
    head = head_ref.shape[0]
    half = d_pre.shape[1] // 2
    head_ref[...] = d_pre[:head, :]
    agg_t = agg.T
    own_t = own.T
    for k in range(swap_ref.shape[0]):
        swap_ref[k, :SHARE, :] = agg_t[k * SHARE : (k + 1) * SHARE, :]
        swap_ref[k, SHARE : 2 * SHARE, :] = own_t[k * SHARE : (k + 1) * SHARE, :]
        swap_ref[k, 2 * SHARE : 2 * SHARE + TAIL, :] = d_pre[head:, :half]
        swap_ref[k, 2 * SHARE + TAIL :, :] = d_pre[head:, half:]


def grad_step(head_ref, swap_ref, out_ref):
    n = swap_ref.shape[0]
    head = head_ref.shape[0] // n
    total = jnp.zeros(out_ref.shape[1:], F32)
    for k in range(n):
        tail = jnp.concatenate(
            [swap_ref[k, 2 * SHARE : 2 * SHARE + TAIL, :], swap_ref[k, 2 * SHARE + TAIL :, :]], axis=1
        )
        d_pre = jnp.concatenate([head_ref[k * head : (k + 1) * head, :], tail], axis=0)
        total += jnp.dot(swap_ref[k, : 2 * SHARE, :], d_pre, preferred_element_type=F32)
    for k in range(out_ref.shape[0]):
        out_ref[k] = total


def repeat_step(one_ref, out_ref):
    one = one_ref[...]
    for k in range(out_ref.shape[0]):
        out_ref[k] = one


def sum_repeat_step(parts_ref, out_ref):
    total = jnp.sum(parts_ref[...], axis=0)
    for k in range(out_ref.shape[0]):
        out_ref[k] = total


def sum_step(parts_ref, out_ref):
    out_ref[...] = jnp.sum(parts_ref[...].astype(F32), axis=0).astype(BF16)


def call(kernel, ins, outs, scratch=()):
    single = not isinstance(outs, list)
    return pl.pallas_call(
        kernel,
        out_shape=outs,
        in_specs=ins,
        out_specs=VMEM if single else [VMEM] * len(outs),
        scratch_shapes=scratch,
        compiler_params=PARAMS,
    )


def repeat_rows(one, n):
    step = max(n // 8, 1)
    return pl.pallas_call(
        repeat_step,
        grid=(n // step,),
        out_shape=jax.ShapeDtypeStruct((n,) + one.shape, one.dtype),
        in_specs=[pl.BlockSpec(one.shape, lambda i: (0, 0))],
        out_specs=pl.BlockSpec((step,) + one.shape, lambda i: (i, 0, 0)),
        compiler_params=PARAMS,
    )(one)


def on_device(
    source_feats, target_feats, w_neigh, w_self, tile_count, tile_rows, tile_cols, tile_vals, cotangent
):
    width = source_feats.shape[1]
    n_x, n_y, n_z = (lax.axis_size(a) for a in ("x", "y", "z"))
    n_col = lax.axis_size(COL)
    n_row = lax.axis_size(ROW)
    own_rows = target_feats.shape[0]
    own_source = source_feats.shape[0]
    sds = jax.ShapeDtypeStruct
    slots = [SMEM, SMEM, SMEM, VMEM]
    rows = RB * TILE

    block_source = lax.all_to_all(
        repeat_rows(source_feats, n_row),
        ROW, 0, 0, tiled=True,
    ).reshape(rows, width)
    core = lax.axis_index("core").astype(jnp.int32).reshape(1, 1)
    mine, send = call(
        forward_tiles, [SMEM] + slots + [VMEM],
        [sds((rows // 2, width), F32), sds((rows // 2, width), BF16)],
        [pltpu.VMEM((rows, width), F32)],
    )(core, tile_count, tile_rows, tile_cols, tile_vals, block_source)
    got = lax.ppermute(send, "core", [(0, 1), (1, 0)])
    pair = (mine + got.astype(F32)).astype(BF16)
    parts = lax.all_to_all(pair, "z", 0, 0, tiled=True)
    layer_out, d_target, head, swap = call(
        dense_step, [VMEM] * 5,
        [sds((own_rows, width), BF16)] * 2
        + [sds((own_rows - TAIL, width), BF16), sds((n_col, 2 * SHARE + 2 * TAIL, own_rows), BF16)],
    )(parts.reshape(n_z, own_rows, width), target_feats, cotangent, w_neigh, w_self)

    swapped = lax.all_to_all(swap, COL, 0, 0, tiled=True)
    heads = lax.all_gather(head, COL, axis=0, tiled=True)
    grads = call(
        grad_step, [VMEM] * 2, sds((n_y, 2 * SHARE, width), F32),
    )(heads, swapped)
    grads = lax.all_to_all(grads, "y", 0, 0, tiled=True)
    grads = call(sum_repeat_step, [VMEM], sds((n_x, 2 * SHARE, width), F32))(grads)
    grads_x = lax.all_to_all(grads, "x", 0, 0, tiled=True)
    source_part = call(
        backward_tiles, slots + [VMEM] * 3 + [pl.BlockSpec(memory_space=pl.ANY)], sds((CB * TILE, width), BF16),
        [pltpu.VMEM((rows, width), BF16)] * 2 + [pltpu.VMEM((CB * TILE, width), F32)],
    )(tile_count, tile_rows, tile_cols, tile_vals, heads, swapped, w_neigh, grads)
    source_parts = lax.all_to_all(source_part, ROW, 0, 0, tiled=True)
    grads = jnp.sum(grads_x, axis=0)
    all_grads = lax.all_gather(grads, COL, axis=0, tiled=False)
    d_source = call(sum_step, [VMEM], sds(source_feats.shape, BF16))(
        source_parts.reshape(n_row, -1, width)
    )
    all_grads = all_grads.reshape(n_col, 2, SHARE, width).swapaxes(0, 1).reshape(2, width, width)
    return (layer_out, d_target, d_source, all_grads[0], all_grads[1])


def solution(mesh):
    n_row, n_col = mesh.devices.shape
    n_y = min(n_row, 8)
    mesh = Mesh(mesh.devices.reshape(n_row // n_y, n_y, n_col // 2, 2), ROW + COL)
    targets = P(ROW + COL, None)
    sources = P(COL + ROW, None)
    in_specs = (
        sources,
        targets,
        P(),
        P(),
        P(ROW, COL),
        P(ROW, COL, None),
        P(ROW, COL, None),
        P(ROW, COL, None, None, None),
        targets,
    )
    out_specs = (targets, targets, sources, P(), P())
    return jax.shard_map(
        on_device, mesh=mesh, in_specs=in_specs, out_specs=out_specs, check_vma=False
    )
```

```python
import jax
import jax.numpy as jnp
from jax import lax
from jax.experimental import pallas as pl
from jax.experimental.pallas import tpu as pltpu
from jax.sharding import Mesh, PartitionSpec as P

RB = 16
CB = 16
TILE = 128
GROUP = 16
REST = 8
SHARE = 16
TAIL = 8
ROW = ("x", "y")
COL = ("z", "core")
F32 = jnp.float32
BF16 = jnp.bfloat16
VMEM = pl.BlockSpec(memory_space=pltpu.VMEM)
SMEM = pl.BlockSpec(memory_space=pltpu.SMEM)
PARAMS = pltpu.CompilerParams(vmem_limit_bytes=32 * 1024 * 1024)


def live_tiles(count, add, product):
    groups = count // GROUP
    done = groups * GROUP

    def group(g, carry):
        for k in range(GROUP):
            s = g * GROUP + k
            add(s, product(s))
        return carry

    def rest(g, carry):
        for k in range(REST):
            s = done + g * REST + k
            add(s, jnp.where(s < count, product(s), 0.0))
        return carry

    lax.fori_loop(0, groups, group, 0)
    lax.fori_loop(0, (count - done + (REST - 1)) // REST, rest, 0)


def forward_tiles(
    core_ref, count_ref, rows_ref, cols_ref, vals_ref, src_ref, mine_ref, send_ref, total
):
    count = count_ref[0, 0]
    total[...] = jnp.zeros_like(total)

    def product(s):
        of = pl.ds(pl.multiple_of(cols_ref[0, 0, s] * TILE, TILE), TILE)
        return jnp.dot(vals_ref[0, 0, s], src_ref[of, :], preferred_element_type=F32)

    def add(s, value):
        at = pl.ds(pl.multiple_of(rows_ref[0, 0, s] * TILE, TILE), TILE)
        total[at, :] += value

    live_tiles(count, add, product)
    core = core_ref[0, 0]
    share = mine_ref.shape[0] // (RB // 2)
    for k in range(RB // 2):
        here = slice(k * share, (k + 1) * share)
        keep = pl.ds(pl.multiple_of((2 * k + core) * share, share), share)
        give = pl.ds(pl.multiple_of((2 * k + 1 - core) * share, share), share)
        mine_ref[here, :] = total[keep, :]
        send_ref[here, :] = total[give, :].astype(BF16)


def assemble(head_ref, swap_ref, d_pre):
    n = swap_ref.shape[0]
    head = head_ref.shape[0] // n
    full = head + TAIL
    half = d_pre.shape[1] // 2
    for k in range(n):
        d_pre[k * full : k * full + head, :] = head_ref[k * head : (k + 1) * head, :]
        rows = slice(k * full + head, (k + 1) * full)
        d_pre[rows, :half] = swap_ref[k, 2 * SHARE : 2 * SHARE + TAIL, :]
        d_pre[rows, half:] = swap_ref[k, 2 * SHARE + TAIL : 2 * SHARE + 2 * TAIL, :]


def backward_tiles(
    count_ref, rows_ref, cols_ref, vals_ref, head_ref, swap_ref, w_neigh_ref, after_ref, out_ref,
    d_pre, d_agg, total,
):
    count = count_ref[0, 0]
    total[...] = jnp.zeros_like(total)
    assemble(head_ref, swap_ref, d_pre)
    d_agg[...] = lax.dot_general(
        d_pre[...], w_neigh_ref[...], (((1,), (1,)), ((), ())), preferred_element_type=F32
    ).astype(BF16)

    def product(s):
        of = pl.ds(pl.multiple_of(rows_ref[0, 0, s] * TILE, TILE), TILE)
        return lax.dot_general(
            vals_ref[0, 0, s], d_agg[of, :], (((0,), (0,)), ((), ())), preferred_element_type=F32
        )

    def add(s, value):
        at = pl.ds(pl.multiple_of(cols_ref[0, 0, s] * TILE, TILE), TILE)
        total[at, :] += value

    live_tiles(count, add, product)
    out_ref[...] = total[...].astype(BF16)


def dense_step(
    parts_ref, own_ref, cot_ref, w_neigh_ref, w_self_ref, out_ref, d_tgt_ref, head_ref, swap_ref
):
    agg = jnp.sum(parts_ref[...].astype(F32), axis=0).astype(BF16)
    own = own_ref[...]
    preact = jnp.dot(agg, w_neigh_ref[...], preferred_element_type=F32) + jnp.dot(
        own, w_self_ref[...], preferred_element_type=F32
    )
    cdf = 0.5 * (1.0 + lax.erf(preact * 0.7071067811865476))
    density = jnp.exp(-0.5 * preact * preact) * 0.3989422804014327
    out_ref[...] = (preact * cdf).astype(BF16)
    d_pre = (cot_ref[...].astype(F32) * (cdf + preact * density)).astype(BF16)
    d_tgt_ref[...] = lax.dot_general(
        d_pre, w_self_ref[...], (((1,), (1,)), ((), ())), preferred_element_type=F32
    ).astype(BF16)
    head = head_ref.shape[0]
    half = d_pre.shape[1] // 2
    head_ref[...] = d_pre[:head, :]
    agg_t = agg.T
    own_t = own.T
    for k in range(swap_ref.shape[0]):
        swap_ref[k, :SHARE, :] = agg_t[k * SHARE : (k + 1) * SHARE, :]
        swap_ref[k, SHARE : 2 * SHARE, :] = own_t[k * SHARE : (k + 1) * SHARE, :]
        swap_ref[k, 2 * SHARE : 2 * SHARE + TAIL, :] = d_pre[head:, :half]
        swap_ref[k, 2 * SHARE + TAIL :, :] = d_pre[head:, half:]


def grad_step(head_ref, swap_ref, out_ref):
    n = swap_ref.shape[0]
    head = head_ref.shape[0] // n
    total = jnp.zeros(out_ref.shape[1:], F32)
    for k in range(n):
        tail = jnp.concatenate(
            [swap_ref[k, 2 * SHARE : 2 * SHARE + TAIL, :], swap_ref[k, 2 * SHARE + TAIL :, :]], axis=1
        )
        d_pre = jnp.concatenate([head_ref[k * head : (k + 1) * head, :], tail], axis=0)
        total += jnp.dot(swap_ref[k, : 2 * SHARE, :], d_pre, preferred_element_type=F32)
    for k in range(out_ref.shape[0]):
        out_ref[k] = total


def repeat_step(one_ref, out_ref):
    one = one_ref[...]
    for k in range(out_ref.shape[0]):
        out_ref[k] = one


def sum_repeat_step(parts_ref, out_ref):
    total = jnp.sum(parts_ref[...], axis=0)
    for k in range(out_ref.shape[0]):
        out_ref[k] = total


def sum_step(parts_ref, out_ref):
    out_ref[...] = jnp.sum(parts_ref[...].astype(F32), axis=0).astype(BF16)


def call(kernel, ins, outs, scratch=()):
    single = not isinstance(outs, list)
    return pl.pallas_call(
        kernel,
        out_shape=outs,
        in_specs=ins,
        out_specs=VMEM if single else [VMEM] * len(outs),
        scratch_shapes=scratch,
        compiler_params=PARAMS,
    )


def repeat_rows(one, n):
    step = max(n // 8, 1)
    return pl.pallas_call(
        repeat_step,
        grid=(n // step,),
        out_shape=jax.ShapeDtypeStruct((n,) + one.shape, one.dtype),
        in_specs=[pl.BlockSpec(one.shape, lambda i: (0, 0))],
        out_specs=pl.BlockSpec((step,) + one.shape, lambda i: (i, 0, 0)),
        compiler_params=PARAMS,
    )(one)


def on_device(
    source_feats, target_feats, w_neigh, w_self, tile_count, tile_rows, tile_cols, tile_vals, cotangent
):
    width = source_feats.shape[1]
    n_x, n_y, n_z = (lax.axis_size(a) for a in ("x", "y", "z"))
    n_col = lax.axis_size(COL)
    n_row = lax.axis_size(ROW)
    own_rows = target_feats.shape[0]
    own_source = source_feats.shape[0]
    sds = jax.ShapeDtypeStruct
    slots = [SMEM, SMEM, SMEM, VMEM]
    rows = RB * TILE

    block_source = lax.all_to_all(
        repeat_rows(source_feats, n_row),
        ROW, 0, 0, tiled=True,
    ).reshape(rows, width)
    core = lax.axis_index("core").astype(jnp.int32).reshape(1, 1)
    mine, send = call(
        forward_tiles, [SMEM] + slots + [VMEM],
        [sds((rows // 2, width), F32), sds((rows // 2, width), BF16)],
        [pltpu.VMEM((rows, width), F32)],
    )(core, tile_count, tile_rows, tile_cols, tile_vals, block_source)
    got = lax.ppermute(send, "core", [(0, 1), (1, 0)])
    pair = (mine + got.astype(F32)).astype(BF16)
    parts = lax.all_to_all(pair, "z", 0, 0, tiled=True)
    layer_out, d_target, head, swap = call(
        dense_step, [VMEM] * 5,
        [sds((own_rows, width), BF16)] * 2
        + [sds((own_rows - TAIL, width), BF16), sds((n_col, 2 * SHARE + 2 * TAIL, own_rows), BF16)],
    )(parts.reshape(n_z, own_rows, width), target_feats, cotangent, w_neigh, w_self)

    swapped = lax.all_to_all(swap, COL, 0, 0, tiled=True)
    heads = lax.all_gather(head, COL, axis=0, tiled=True)
    grads = call(
        grad_step, [VMEM] * 2, sds((n_y, 2 * SHARE, width), F32),
    )(heads, swapped)
    grads = lax.all_to_all(grads, "y", 0, 0, tiled=True)
    grads = call(sum_repeat_step, [VMEM], sds((n_x, 2 * SHARE, width), F32))(grads)
    grads_x = lax.all_to_all(grads, "x", 0, 0, tiled=True)
    source_part = call(
        backward_tiles, slots + [VMEM] * 3 + [pl.BlockSpec(memory_space=pl.ANY)], sds((CB * TILE, width), BF16),
        [pltpu.VMEM((rows, width), BF16)] * 2 + [pltpu.VMEM((CB * TILE, width), F32)],
    )(tile_count, tile_rows, tile_cols, tile_vals, heads, swapped, w_neigh, grads)
    source_parts = lax.all_to_all(source_part, ROW, 0, 0, tiled=True)
    grads = jnp.sum(grads_x, axis=0)
    all_grads = lax.all_gather(grads, COL, axis=0, tiled=False)
    d_source = call(sum_step, [VMEM], sds(source_feats.shape, BF16))(
        source_parts.reshape(n_row, -1, width)
    )
    all_grads = all_grads.reshape(n_col, 2, SHARE, width).swapaxes(0, 1).reshape(2, width, width)
    return (layer_out, d_target, d_source, all_grads[0], all_grads[1])


def solution(mesh):
    n_row, n_col = mesh.devices.shape
    n_y = min(n_row, 8)
    mesh = Mesh(mesh.devices.reshape(n_row // n_y, n_y, n_col // 2, 2), ROW + COL)
    targets = P(ROW + COL, None)
    sources = P(COL + ROW, None)
    in_specs = (
        sources,
        targets,
        P(),
        P(),
        P(ROW, COL),
        P(ROW, COL, None),
        P(ROW, COL, None),
        P(ROW, COL, None, None, None),
        targets,
    )
    out_specs = (targets, targets, sources, P(), P())
    return jax.shard_map(
        on_device, mesh=mesh, in_specs=in_specs, out_specs=out_specs, check_vma=False
    )
```
